32 devices in a mesh: groups: 2 (over y), wide: 4 (over z), narrow: 4 (over x, core).
Axes of the slice: x: 2, y: 2, z: 4, core: 2. Of those that a mesh axis runs over, the one named last changes fastest.
Arguments:
- hidden: bfloat16 [4096, 4096], P(('groups', 'wide')), parts along dimension 0, may hold values from -16 to 16
- w_qkv: bfloat16 [4096, 3, 2048], P('wide', None, 'narrow'), may hold values from -0.09375 to 0.09375
- w_out: bfloat16 [2048, 4096], P(None, 'wide'), may hold values from -0.125 to 0.125
- seg_ids: int32 [4096], P('groups'), parts along dimension 0, may hold values from 0 to 3, never falling along the last dimension, each value on 1 to 1024 neighbouring positions
- shift_heads: int32 [16], replicated, may hold values from 0 to 1, as said below
Outputs:
- layer_out: bfloat16 [4096, 4096], P(('groups', 'wide', 'narrow')), parts along dimension 0
The draws below stay inside these ranges and needn't reach their ends.
There are 2 independent parts, one for each index of `groups`. The reference program is written for one: setup_inputs(seed, part) draws one part's arguments, and reference() takes and returns one part's arrays. A program takes and returns all parts, laid end to end along the dimension named above; an argument that names none is the same for every part. Nothing has to cross between parts.
Inputs may be any that keep to these rules, and one draw needn't show every extreme that they name: `shift_heads`: exactly half of the heads are marked with 1, the others with 0. `seg_ids`: never falls along the window; every number occurs on 1 to 1024 consecutive tokens, one on exactly that many.
All inputs are finite; a program needn't handle non-finite values.
Results may differ from the reference program's by a relative error of at most 0.012.
Values may be sent and summed in bfloat16 or wider, within the bound.
No kernel may reach another device: no remote copies, remote signals or barrier semaphores. Data moves between devices by JAX's collectives and lax.ppermute only.
A program may use at most 128 MiB of HBM per device.

```python
import math
import jax
import jax.numpy as jnp
import numpy as np
from jax import lax

D = 4096
HEAD_DIM = 128
HEADS = 16
GROUP = 512
SHIFT = 256
TOK_DEV = 512
TOKENS = 2048
N_WIDE = 4


def draw_hidden(key, part):
    first_key = jax.random.fold_in(jax.random.fold_in(key, 11), 0)
    result = jnp.clip(jax.random.normal(first_key, (TOKENS, D), jnp.float32), -6.0, 6.0)
    return result.astype(jnp.bfloat16)


def draw_shift_heads(key, part):
    order = jax.random.permutation(jax.random.fold_in(key, 23), HEADS)
    return (order < HEADS // 2).astype(jnp.int32)


def levels(own_key, extent, cuts, least, largest):
    def one(dim, parts):
        steps = jax.random.uniform(jax.random.fold_in(jax.random.fold_in(own_key, 6), dim), (parts,), jnp.float32, least / len(cuts), largest / len(cuts))
        return jnp.repeat(jnp.exp(steps), extent[dim] // parts).reshape((-1,) + (1,) * (len(extent) - dim - 1))

    loudness = one(*cuts[0])
    for cut in cuts[1:]:
        loudness = loudness * one(*cut)
    return loudness


def split_up(number_of, total, most, lean):
    loads = [(1 << 20) // math.isqrt(standing ** lean) + 1 for standing in range(2, number_of + 1)]
    surplus, holding = total - most - (number_of - 1), [1] * (number_of - 1)
    while surplus > 0:
        candidates = [i for i in range(number_of - 1) if holding[i] < most]
        mass, left = sum([loads[i] for i in candidates]), surplus
        for i in candidates:
            more = min(most - holding[i], max(1, left * loads[i] // mass), surplus)
            holding[i] = holding[i] + more
            surplus = surplus - more
    return np.array([most] + holding)


def uneven_parts(key, count, total, limit, slope):
    if count == 2:
        one = jax.random.randint(key, (), max(1, total - limit), min(limit, total - 1) + 1)
        return jnp.stack([one, total - one])
    sizes = jnp.asarray(split_up(count, total, limit, slope), jnp.int32)
    couples = (count - 1) // 2
    giver, taker = sizes[1:1 + 2 * couples:2], sizes[2:2 + 2 * couples:2]
    slack = jnp.minimum(giver - 1, limit - taker)
    passed = jax.random.randint(jax.random.fold_in(key, 1), (couples,), 0, 1 << 20) % (slack + 1)
    sizes = sizes.at[1:1 + 2 * couples:2].set(giver - passed).at[2:2 + 2 * couples:2].set(taker + passed)
    return sizes[jax.random.permutation(jax.random.fold_in(key, 2), count)]


def centred(own_key, extent, spread, bound, cuts=(), kind=jnp.bfloat16):
    factor_of = levels(own_key, extent, cuts, -0.22, 0.18) if cuts else 1.0
    values = jax.random.normal(own_key, extent, jnp.float32) * spread * factor_of
    return jnp.minimum(jnp.maximum(values, -bound), bound).astype(kind)


def setup_inputs(seed: int = 0, part: int = 0) -> dict:
    keys = jax.random.split(jax.random.key(seed), 6)
    own_keys = jax.random.split(jax.random.fold_in(keys[5], part), 6)
    hidden = draw_hidden(jax.random.fold_in(jax.random.fold_in(keys[5], part), 71), part)
    w_qkv = centred(keys[1], (D, 3, HEADS * HEAD_DIM), D ** -0.5, 0.09375, ((0, 4), (2, 4)))
    w_out = centred(keys[2], (HEADS * HEAD_DIM, D), (HEADS * HEAD_DIM) ** -0.5, 0.125, ((1, 4),))
    seg_ids = jnp.searchsorted(jnp.cumsum(uneven_parts(own_keys[3], N_WIDE, TOKENS, 2 * TOK_DEV, 2)), jnp.arange(TOKENS), side="right").astype(jnp.int32)
    shift_heads = draw_shift_heads(jax.random.fold_in(keys[5], 71), part)
    return dict(hidden=hidden, w_qkv=w_qkv, w_out=w_out, seg_ids=seg_ids, shift_heads=shift_heads)


masked_out = -1e+30

def attend(query_rows, key_rows, value_rows, allowed):
    scores = jnp.einsum('ihd,jhd->hij', query_rows.astype(jnp.float32), key_rows.astype(jnp.float32)) * (1.0 / math.sqrt(HEAD_DIM))
    scores = jnp.where(allowed, scores, masked_out)
    row_max = lax.optimization_barrier(jnp.max(scores, axis=-1, keepdims=True))
    exponent = jnp.exp(scores - row_max)
    weights = (exponent / lax.optimization_barrier(jnp.sum(exponent, axis=-1, keepdims=True))).astype(jnp.bfloat16)
    combined = jnp.einsum('hij,jhd->ihd', weights.astype(jnp.float32), value_rows.astype(jnp.float32))
    return combined.astype(jnp.bfloat16)

def reference(hidden, w_qkv, w_out, seg_ids, shift_heads):
    width = HEADS * HEAD_DIM
    projected = jnp.dot(hidden, w_qkv.reshape(D, 3 * width), preferred_element_type=jnp.float32).astype(jnp.bfloat16)
    projected = projected.reshape(TOKENS, 3, HEADS, HEAD_DIM)
    shifted = shift_heads > 0
    moved_qkv = jnp.where(shifted[None, None, :, None], jnp.roll(projected, -SHIFT, axis=0), projected)
    seg_heads = jnp.where(shifted[:, None], jnp.roll(seg_ids, -SHIFT)[None, :], seg_ids[None, :])
    groups_all = TOKENS // GROUP
    blocks = moved_qkv.reshape(groups_all, GROUP, 3, HEADS, HEAD_DIM)
    block_segs = seg_heads.reshape(HEADS, groups_all, GROUP).transpose(1, 0, 2)
    positions = jnp.arange(GROUP, dtype=jnp.int32)
    causal = positions[:, None] >= positions[None, :]

    def one_group(inputs):
        block_qkv, block_seg = inputs
        allowed = causal[None] & (block_seg[:, :, None] == block_seg[:, None, :])
        return attend(block_qkv[:, 0], block_qkv[:, 1], block_qkv[:, 2], allowed)
    rolled_out = lax.map(one_group, (blocks, block_segs)).reshape(TOKENS, HEADS, HEAD_DIM)
    attended = jnp.where(shifted[None, :, None], jnp.roll(rolled_out, SHIFT, axis=0), rolled_out)
    return jnp.dot(attended.reshape(TOKENS, width), w_out, preferred_element_type=jnp.float32).astype(jnp.bfloat16)
```

```python
import math

import jax
import jax.numpy as jnp
from jax import lax
from jax.sharding import PartitionSpec as P

HEAD_DIM = 128
GROUP = 512
SHIFT = 256
CHUNK_ROWS = 512

masked_out = -1e30


def swap(block, axis, mask):
    return lax.ppermute(block, axis, [(i, i ^ mask) for i in range(lax.axis_size(axis))])


def narrow_masks():
    masks = []
    mask = lax.axis_size("narrow") // 2
    while mask:
        masks.append(mask)
        mask //= 2
    return masks


def widen(stack, steps):
    for axis, mask in steps:
        stack = jnp.concatenate([stack, swap(stack, axis, mask)], 0)
    return stack


def line_step(block, step, direction):
    size = lax.axis_size("wide")
    if direction > 0:
        route = [(i, i + 1) for i in range(step - 1, size - 1)]
    else:
        route = [(i, i - 1) for i in range(1, size - step + 1)]
    return lax.ppermute(block, "wide", route)


def attend(query, key, value, allowed):
    scores = jnp.einsum("gbihd,gbjhd->gbhij", query, key, preferred_element_type=jnp.float32)
    scores = scores * (1.0 / math.sqrt(HEAD_DIM))
    scores = jnp.where(allowed, scores, masked_out)
    row_max = jnp.max(scores, axis=-1, keepdims=True)
    exponent = jnp.exp(scores - row_max)
    weights = (exponent / jnp.sum(exponent, axis=-1, keepdims=True)).astype(jnp.bfloat16)
    combined = jnp.einsum("gbhij,gbjhd->gbihd", weights, value, preferred_element_type=jnp.float32)
    return combined.astype(jnp.bfloat16)


def per_device(hidden, w_qkv, w_out, seg_ids, shift_heads):
    tok_rows, depth = hidden.shape
    wide, narrow, groups = lax.axis_size("wide"), lax.axis_size("narrow"), lax.axis_size("groups")
    wide_idx, narrow_idx, group_idx = (lax.axis_index(a) for a in ("wide", "narrow", "groups"))
    in_rows, _, block_f = w_qkv.shape
    local_f = block_f // groups
    heads_here = local_f // HEAD_DIM
    plane = narrow * groups
    masks = narrow_masks()
    plane_steps = [("groups", 1)] + [("narrow", m) for m in masks]

    out_piece = lax.dynamic_slice_in_dim(w_out, (narrow_idx * groups + group_idx) * local_f, local_f, 0)
    out_up, out_down = {}, {}
    up = down = out_piece
    for step in range(1, wide):
        up, down = line_step(up, step, 1), line_step(down, step, -1)
        out_up[step], out_down[step] = up, down

    quarter = tok_rows // narrow
    other_part = swap(lax.dynamic_slice_in_dim(hidden, narrow_idx * quarter, quarter, 0), "groups", 1)
    halo_rows = SHIFT // narrow
    halo_part = lax.ppermute(
        lax.dynamic_slice_in_dim(hidden, tok_rows - SHIFT + narrow_idx * halo_rows, halo_rows, 0),
        "wide",
        [(i, (i + 1) % wide) for i in range(wide)],
    )
    halo_other = swap(halo_part, "groups", 1)
    stack = jnp.concatenate([other_part, halo_part, halo_other], 0)[None]
    stack = widen(stack, [("narrow", m) for m in masks])

    def entry_of(distance):
        return sum(((distance // m) % 2) * (1 << k) for k, m in enumerate(masks))

    ordered = jnp.concatenate(
        [lax.dynamic_slice_in_dim(stack, entry_of(narrow_idx ^ j), 1, 0) for j in range(narrow)], 0
    )
    other = ordered[:, :quarter].reshape(tok_rows, depth)
    halo_own = ordered[:, quarter : quarter + halo_rows].reshape(SHIFT, depth)
    halo_oth = ordered[:, quarter + halo_rows :].reshape(SHIFT, depth)
    rows = jnp.concatenate([halo_own, hidden, halo_oth, other], 0)

    own_w = lax.dynamic_slice_in_dim(w_qkv, group_idx * local_f, local_f, 2)
    own_w = jnp.concatenate([own_w[:, 0], own_w[:, 1], own_w[:, 2]], 1)
    size = min(in_rows, CHUNK_ROWS)
    chunks = in_rows // size
    ups = [own_w[c * size : (c + 1) * size] for c in range(chunks)]
    downs = list(ups)

    def product(block, owner, c):
        columns = lax.dynamic_slice_in_dim(rows, owner * in_rows + c * size, size, 1)
        return jnp.dot(columns, block, preferred_element_type=jnp.float32)

    total = None
    for c in range(chunks):
        part = product(ups[c], wide_idx, c)
        total = part if total is None else total + part
    for step in range(1, wide):
        for c in range(chunks):
            ups[c] = line_step(ups[c], step, 1)
            downs[c] = line_step(downs[c], step, -1)
            below, above = wide_idx - step, wide_idx + step
            if 2 * step <= wide - 1:
                total = total + product(ups[c], jnp.maximum(below, 0), c)
                total = total + product(downs[c], jnp.minimum(above, wide - 1), c)
            else:
                from_below = below >= 0
                block = jnp.where(from_below, ups[c], downs[c])
                owner = jnp.where(from_below, below, jnp.minimum(above, wide - 1))
                total = total + product(block, owner, c)
            total = lax.optimization_barrier(total)
    projected = total.astype(jnp.bfloat16).reshape(2, SHIFT + tok_rows, 3, heads_here, HEAD_DIM)

    blocks = tok_rows // SHIFT
    first_tok = wide_idx * tok_rows
    segs = jnp.stack([seg_ids, swap(seg_ids, "groups", 1)])
    looped = jnp.concatenate([segs[:, -SHIFT:], segs], 1)
    segs = lax.dynamic_slice_in_dim(looped, first_tok, SHIFT + tok_rows, 1)
    shifted = lax.dynamic_slice_in_dim(
        shift_heads, (narrow_idx * groups + group_idx) * heads_here, heads_here
    )

    def windows(array):
        return jnp.stack([array[:, b * SHIFT : (b + 2) * SHIFT] for b in range(blocks)], 1)

    query = projected[:, SHIFT:, 0].reshape(2, blocks, SHIFT, heads_here, HEAD_DIM)
    key, value = windows(projected[:, :, 1]), windows(projected[:, :, 2])
    seg_query, seg_key = segs[:, SHIFT:].reshape(2, blocks, SHIFT), windows(segs)
    same = seg_query[:, :, None, :, None] == seg_key[:, :, None, None, :]
    i = jnp.arange(SHIFT, dtype=jnp.int32)[:, None]
    j = jnp.arange(2 * SHIFT, dtype=jnp.int32)[None, :] - SHIFT
    half = jnp.arange(blocks, dtype=jnp.int32)[:, None] % (GROUP // SHIFT)
    joined = half != shifted[None, :]
    allowed = same & (((j >= 0) & (j <= i)) | ((j < 0) & joined[None, :, :, None, None]))
    attended = attend(query, key, value, allowed).reshape(2, tok_rows, local_f)

    out_rows = tok_rows // narrow
    pieces, own_out = [], []
    for e in range(plane):
        a, m = e % 2, sum(mk for k, mk in enumerate(masks) if (e >> (k + 1)) & 1)
        part = lax.dynamic_slice_in_dim(attended[a], (narrow_idx ^ m) * out_rows, out_rows, 0)
        if e:
            route = [(d, d ^ (a * narrow + m)) for d in range(plane)]
            part = lax.ppermute(part, ("groups", "narrow"), route)
        pieces.append(part)
        start = ((narrow_idx ^ m) * groups + (group_idx ^ a)) * local_f
        own_out.append(lax.dynamic_slice_in_dim(w_out, start, local_f, 0))
    mine = jnp.concatenate(pieces, 1)
    results = [jnp.dot(mine, jnp.concatenate(own_out, 0), preferred_element_type=jnp.float32)]
    for d in range(1, wide):
        piece = jnp.where(wide_idx + d < wide, out_down[d], out_up[wide - d])
        half_stack = widen(piece[None], plane_steps[:-1]).reshape(-1, piece.shape[1])
        rest = swap(half_stack, *plane_steps[-1])
        cut = half_stack.shape[0]
        results.append(
            jnp.dot(mine[:, :cut], half_stack, preferred_element_type=jnp.float32)
            + jnp.dot(mine[:, cut:], rest, preferred_element_type=jnp.float32)
        )
    relative = jnp.concatenate([r.astype(jnp.bfloat16) for r in results], 1)
    twice = jnp.concatenate([relative, relative], 1)
    columns = relative.shape[1] // wide
    return lax.dynamic_slice_in_dim(twice, (wide - wide_idx) * columns, relative.shape[1], 1)


def solution(mesh):
    placed = (
        P(("groups", "wide"), None),
        P("wide", None, "narrow"),
        P(None, "wide"),
        P("groups"),
        P(),
    )
    return jax.shard_map(
        per_device,
        mesh=mesh,
        in_specs=placed,
        out_specs=P(("groups", "wide", "narrow"), None),
        check_vma=False,
    )
```

```python
import functools
import math

import jax
import jax.numpy as jnp
from jax import lax
from jax.experimental import pallas as pl
from jax.experimental.pallas import tpu as pltpu
from jax.sharding import PartitionSpec as P

HEAD_DIM = 128
GROUP = 512
SHIFT = 256
CHUNK_ROWS = 512

masked_out = -1e30


def after(block, *earlier):
    return lax.optimization_barrier((block, *earlier))[0]


class Lane:
    def __init__(self, depth=2):
        self.depth, self.ended = depth, []

    def send(self, block, axis, route, *earlier):
        if len(self.ended) >= self.depth:
            earlier = (*earlier, self.ended[-self.depth])
        if earlier:
            block = after(block, *earlier)
        result = lax.ppermute(block, axis, route)
        self.ended.append(result)
        return result


def xor_route(size, mask):
    return [(i, i ^ mask) for i in range(size)]


def attend_kernel(
    theirs_turn, blocks, heads, flags, row_seg, col_seg, own, other, part0, part1, halo, out, rows
):
    second, side = flags[0], flags[1]
    narrow = (flags.shape[0] - 2 - heads) // 2
    half = part0.shape[0] // 4
    quarter = other.shape[0] // narrow
    halo_rows = halo.shape[0] // (2 * narrow)
    tok_rows = own.shape[0]

    def fetch_mine(group, start, count, to):
        if group == 0:
            rows[group, to : to + count] = own[start : start + count]
        else:
            for b in range(start // quarter, (start + count) // quarter):
                at = to + b * quarter - start
                place = pl.multiple_of(flags[2 + b] * quarter, quarter)
                rows[group, at : at + quarter] = other[pl.ds(place, quarter)]

    def fetch_theirs(group, start, count, to):
        for b in range(start // half, (start + count) // half):
            at = to + b * half - start
            place = (b // 2) ^ side
            place = pl.multiple_of((place * 2 + group) * half, half)
            rows[group, at : at + half] = (part0, part1)[b % 2][pl.ds(place, half)]

    def fetch_halo(group):
        for b in range(narrow):
            place = flags[2 + narrow + b] * 2 + group
            place = pl.multiple_of(place * halo_rows, halo_rows)
            rows[group, b * halo_rows : (b + 1) * halo_rows] = halo[pl.ds(place, halo_rows)]

    here, there = (fetch_theirs, fetch_mine) if theirs_turn else (fetch_mine, fetch_theirs)
    first = second == 1 if theirs_turn else second == 0
    for group in range(2):
        here(group, 0, tok_rows, SHIFT)

    @pl.when(first)
    def _():
        for group in range(2):
            fetch_halo(group)

    @pl.when(jnp.logical_not(first))
    def _():
        for group in range(2):
            there(group, tok_rows - SHIFT, SHIFT, 0)

    i = lax.broadcasted_iota(jnp.int32, (SHIFT, 2 * SHIFT), 0)
    j = lax.broadcasted_iota(jnp.int32, (SHIFT, 2 * SHIFT), 1) - SHIFT
    width = heads * HEAD_DIM
    for group in range(2):
        for b in range(blocks):
            span = slice(b * SHIFT, (b + 2) * SHIFT)
            same = col_seg[group, (b + 1) * SHIFT : (b + 2) * SHIFT] == row_seg[group, :, span]
            causal = same & (j >= 0) & (j <= i)
            whole = same & (j < 0)
            for h in range(heads):
                joined = flags[2 + 2 * narrow + h] != b % (GROUP // SHIFT)
                allowed = causal | (whole & joined)
                lanes = slice(h * HEAD_DIM, (h + 1) * HEAD_DIM)
                query = rows[group, (b + 1) * SHIFT : (b + 2) * SHIFT, lanes]
                key = rows[group, span, width + h * HEAD_DIM : width + (h + 1) * HEAD_DIM]
                value = rows[group, span, 2 * width + h * HEAD_DIM : 2 * width + (h + 1) * HEAD_DIM]
                scores = lax.dot_general(
                    query, key, (((1,), (1,)), ((), ())), preferred_element_type=jnp.float32
                ) * (1.0 / math.sqrt(HEAD_DIM))
                scores = jnp.where(allowed, scores, masked_out)
                exponent = jnp.exp(scores - jnp.max(scores, axis=-1, keepdims=True))
                total = jnp.sum(exponent, axis=-1, keepdims=True)
                weights = (exponent / total).astype(jnp.bfloat16)
                combined = jnp.dot(weights, value, preferred_element_type=jnp.float32)
                out[group, b * SHIFT : (b + 1) * SHIFT, lanes] = combined.astype(jnp.bfloat16)


def attend(theirs_turn, flags, segs, heads, own, *others):
    tok_rows, features = own.shape
    vmem, smem = pl.BlockSpec(memory_space=pltpu.VMEM), pl.BlockSpec(memory_space=pltpu.SMEM)
    body = functools.partial(attend_kernel, theirs_turn, tok_rows // SHIFT, heads)
    flops = 2 * tok_rows * 2 * SHIFT * HEAD_DIM * heads * 4
    return pl.pallas_call(
        body,
        out_shape=jax.ShapeDtypeStruct((2, tok_rows, heads * HEAD_DIM), jnp.bfloat16),
        in_specs=[smem] + [vmem] * 7,
        out_specs=vmem,
        scratch_shapes=[pltpu.VMEM((2, SHIFT + tok_rows, features), jnp.bfloat16)],
        compiler_params=pltpu.CompilerParams(vmem_limit_bytes=48 << 20),
        cost_estimate=pl.CostEstimate(flops=flops, bytes_accessed=8 << 20, transcendentals=0),
    )(flags, segs[:, None, :], segs[:, :, None], own, *others)


def reorder(pieces, table, rows):
    count, width = table.shape[0], pieces.shape[1]

    def body(table, piece, out):
        out[...] = piece[...]

    return pl.pallas_call(
        body,
        out_shape=jax.ShapeDtypeStruct((rows, count * width), pieces.dtype),
        grid_spec=pltpu.PrefetchScalarGridSpec(
            num_scalar_prefetch=1,
            grid=(count,),
            in_specs=[pl.BlockSpec((rows, width), lambda e, table: (table[e], 0))],
            out_specs=pl.BlockSpec((rows, width), lambda e, table: (0, e)),
        ),
    )(table, pieces)


def per_device(hidden, w_qkv, w_out, seg_ids, shift_heads):
    tok_rows, depth = hidden.shape
    wide, narrow, groups = lax.axis_size("wide"), lax.axis_size("narrow"), lax.axis_size("groups")
    wide_idx, narrow_idx, group_idx = (lax.axis_index(a) for a in ("wide", "narrow", "groups"))
    in_rows, _, block_f = w_qkv.shape
    local_f = block_f // groups
    heads_here = local_f // HEAD_DIM
    plane = narrow * groups
    masks = [narrow >> (k + 1) for k in range(narrow.bit_length() - 1)]
    y_route = xor_route(groups, 1)

    def rel(e, steps):
        return sum(m for k, m in enumerate(steps) if (e >> k) & 1)

    pairs = wide // 2
    worker = [2 * p + 1 if 2 * p < pairs else 2 * p for p in range(pairs)]
    inward = [(w ^ 1, w) for w in worker]
    outward = [(w, w ^ 1) for w in worker]
    ring = [(worker[p], worker[(p + 1) % pairs]) for p in range(pairs)]
    before = [((2 * p - 1) % wide, worker[p]) for p in range(pairs)]
    pair_idx = wide_idx // 2
    worker_of = jnp.array(worker, jnp.int32)
    i_work = worker_of[pair_idx] == wide_idx

    mid, end, ylane, xlane, core = Lane(), Lane(), Lane(), Lane(), Lane()

    quarter, halo_rows = tok_rows // narrow, SHIFT // narrow
    half = tok_rows // 2
    side = narrow_idx % 2

    def rows_of(start, count):
        return lax.dynamic_slice_in_dim(hidden, start, count, 0)

    other_q = ylane.send(rows_of(narrow_idx * quarter, quarter), "groups", y_route)
    halo_q = mid.send(
        rows_of(tok_rows - SHIFT + narrow_idx * halo_rows, halo_rows), "wide", before
    )
    partner = [None, None]
    part = half // 2
    partner[0] = end.send(rows_of(side * half, part), "wide", inward)

    own_w = lax.dynamic_slice_in_dim(w_qkv, group_idx * local_f, local_f, 2)
    own_w = jnp.concatenate([own_w[:, 0], own_w[:, 1], own_w[:, 2]], 1)
    size = min(in_rows, CHUNK_ROWS)
    chunks = in_rows // size
    own_chunks = [own_w[c * size : (c + 1) * size] for c in range(chunks)]

    arrived = [(wide_idx, c, own_chunks[c]) for c in range(chunks)]
    held_own = [mid.send(b, "wide", ring) for b in own_chunks]
    held_end = []
    for c in range(chunks):
        held_end.append(end.send(own_chunks[c], "wide", inward))
        if c == 0:
            partner[1] = end.send(rows_of(side * half + part, part), "wide", inward)
    end_w = list(held_end)

    other = other_q[None]
    for m in masks:
        lane = core if m == 1 else xlane
        other = jnp.concatenate([other, lane.send(other, "narrow", xor_route(narrow, m))], 0)

    halos = jnp.stack([halo_q, ylane.send(halo_q, "groups", y_route)])[None]
    partner_sets = []
    for j in range(2):
        both = jnp.stack([partner[j], ylane.send(partner[j], "groups", y_route)])[None]
        if j == 0:
            for m in masks:
                lane = core if m == 1 else xlane
                halos = jnp.concatenate([halos, lane.send(halos, "narrow", xor_route(narrow, m))], 0)
        both = jnp.concatenate([both, core.send(both, "narrow", xor_route(narrow, 1))], 0)
        partner_sets.append(both)

    for c in range(chunks):
        arrived.append(((wide_idx ^ 1), c, end_w[c]))
    for step in range(1, pairs):
        source = worker_of[(pair_idx - step) % pairs]
        if step > 1:
            held_own = [mid.send(b, "wide", ring) for b in held_own]
        for c in range(chunks):
            arrived.append((source, c, held_own[c]))
        held_end = [mid.send(b, "wide", ring) for b in held_end]
        for c in range(chunks):
            arrived.append((source ^ 1, c, held_end[c]))

    out_piece = lax.dynamic_slice_in_dim(w_out, (narrow_idx * groups + group_idx) * local_f, local_f, 0)
    slots = []
    up = down = after(out_piece, mid.ended[-2])
    for step in range(1, wide):
        up = lax.ppermute(up, "wide", [(i, i + 1) for i in range(step - 1, wide - 1)])
        down = lax.ppermute(down, "wide", [(i, i - 1) for i in range(1, wide - step + 1)])
        below, above = wide_idx - step, wide_idx + step
        below = jnp.where(below >= 0, below, wide)
        above = jnp.where(above < wide, above, wide)
        if 2 * step <= wide - 1:
            slots += [(above, down), (below, up)]
        else:
            slots.append((jnp.minimum(above, below), jnp.where(above < wide, down, up)))
    out_blocks = []
    for place, piece in slots:
        stack = jnp.concatenate([piece[None], ylane.send(piece[None], "groups", y_route)], 0)
        for m in masks[:-1]:
            stack = jnp.concatenate([stack, xlane.send(stack, "narrow", xor_route(narrow, m))], 0)
        stack = stack.reshape(-1, piece.shape[1])
        out_blocks.append((place, stack, core.send(stack, "narrow", xor_route(narrow, masks[-1]))))

    def project(rows):
        flat = rows.reshape(-1, depth)
        total = None
        for owner, c, block in arrived:
            columns = lax.dynamic_slice_in_dim(flat, owner * in_rows + c * size, size, 1)
            product = jnp.dot(columns, block, preferred_element_type=jnp.float32)
            total = product if total is None else lax.optimization_barrier(total + product)
        return total.astype(jnp.bfloat16)

    def place_rows(blocks, index_of):
        count = blocks.shape[0]
        out = jnp.zeros_like(blocks)
        for e in range(count):
            out = lax.dynamic_update_slice_in_dim(out, blocks[e : e + 1], index_of[e], 0)
        return out.reshape(-1, blocks.shape[-1])

    features = own_w.shape[1]
    near = [narrow_idx ^ rel(e, masks) for e in range(narrow)]
    sets = [project(r) for r in (hidden, other, *partner_sets, halos)]

    segs = jnp.stack([seg_ids, lax.ppermute(seg_ids, "groups", y_route)])
    segs = jnp.concatenate([segs[:, -SHIFT:], segs], 1)
    shifted = lax.dynamic_slice_in_dim(
        shift_heads, (narrow_idx * groups + group_idx) * heads_here, heads_here
    )
    second = wide_idx % 2

    def entry_of(distance):
        return sum(((distance // m) % 2) * (1 << k) for k, m in enumerate(masks))

    entries = jnp.stack([entry_of(narrow_idx ^ b) for b in range(narrow)])
    flags = jnp.concatenate(
        [jnp.stack([second, side]), entries, entries, (shifted > 0).astype(jnp.int32)]
    ).astype(jnp.int32)

    def attended_from(theirs_turn, start):
        start = pair_idx * 2 * tok_rows + start
        seg = lax.dynamic_slice_in_dim(segs, start, SHIFT + tok_rows, 1)
        return attend(theirs_turn, flags, seg, heads_here, *sets)

    att_theirs = attended_from(True, (1 - second) * tok_rows)
    att_back = lax.ppermute(att_theirs, "wide", outward)
    att_mine = attended_from(False, second * tok_rows)
    attended = jnp.where(i_work, att_mine, att_back)

    out_rows = tok_rows // narrow
    steps = [narrow] + masks
    to_all = attended.reshape(2, narrow, out_rows, local_f)
    to_all = jnp.where(group_idx == 0, to_all, to_all[::-1]).reshape(plane * out_rows, local_f)
    from_all = lax.all_to_all(to_all, ("groups", "narrow"), 0, 0, tiled=True)
    self_idx = group_idx * narrow + narrow_idx
    table = jnp.stack([self_idx ^ rel(e, steps) for e in range(plane)]).astype(jnp.int32)
    mine_all = reorder(from_all, table, out_rows)
    in_order = from_all.reshape(groups, narrow, out_rows, local_f).transpose(2, 1, 0, 3)
    columns = w_out.shape[1]
    result = jnp.zeros((out_rows, (wide + 1) * columns), jnp.bfloat16)

    def put(result, value, place):
        return lax.dynamic_update_slice_in_dim(
            result, value.astype(jnp.bfloat16), place * columns, 1
        )

    own_part = jnp.dot(in_order.reshape(out_rows, -1), w_out, preferred_element_type=jnp.float32)
    result = put(result, own_part, wide_idx)
    for place, first, rest in out_blocks:
        cut = first.shape[0]
        value = jnp.dot(mine_all[:, :cut], first, preferred_element_type=jnp.float32)
        value = value + jnp.dot(mine_all[:, cut:], rest, preferred_element_type=jnp.float32)
        result = put(result, value, place)
    return result[:, : wide * columns]


def solution(mesh):
    placed = (
        P(("groups", "wide"), None),
        P("wide", None, "narrow"),
        P(None, "wide"),
        P("groups"),
        P(),
    )
    return jax.shard_map(
        per_device,
        mesh=mesh,
        in_specs=placed,
        out_specs=P(("groups", "wide", "narrow"), None),
        check_vma=False,
    )
```

```python
import functools
import math

import jax
import jax.numpy as jnp
from jax import lax
from jax.experimental import pallas as pl
from jax.experimental.pallas import tpu as pltpu
from jax.sharding import PartitionSpec as P

HEAD_DIM = 128
GROUP = 512
SHIFT = 256
CHUNK_ROWS = 512

masked_out = -1e30


def after(block, *earlier):
    return lax.optimization_barrier((block, *earlier))[0]


def send(block, axis, route, *earlier):
    if earlier:
        block = after(block, *earlier)
    return lax.ppermute(block, axis, route)


def xor_route(size, mask):
    return [(i, i ^ mask) for i in range(size)]


def attend_kernel(blocks, heads, flags, row_seg, col_seg, own, other, halo, out, rows):
    narrow = flags.shape[0] - 1 - heads
    tok_rows = own.shape[0]
    half = tok_rows // 2
    halo_rows = SHIFT // narrow
    for group in range(2):
        for b in range(narrow):
            place = pl.multiple_of((flags[1 + b] * 2 + group) * halo_rows, halo_rows)
            rows[group, b * halo_rows : (b + 1) * halo_rows] = halo[pl.ds(place, halo_rows)]
    rows[0, SHIFT:] = own[...]
    for b in range(2):
        place = pl.multiple_of((b ^ flags[0]) * half, half)
        rows[1, SHIFT + b * half : SHIFT + (b + 1) * half] = other[pl.ds(place, half)]

    i = lax.broadcasted_iota(jnp.int32, (SHIFT, 2 * SHIFT), 0)
    j = lax.broadcasted_iota(jnp.int32, (SHIFT, 2 * SHIFT), 1) - SHIFT
    width = heads * HEAD_DIM
    for group in range(2):
        for b in range(blocks):
            span = slice(b * SHIFT, (b + 2) * SHIFT)
            same = col_seg[group, (b + 1) * SHIFT : (b + 2) * SHIFT] == row_seg[group, :, span]
            causal = same & (j >= 0) & (j <= i)
            whole = same & (j < 0)
            for h in range(heads):
                joined = flags[1 + narrow + h] != b % (GROUP // SHIFT)
                allowed = causal | (whole & joined)
                lanes = slice(h * HEAD_DIM, (h + 1) * HEAD_DIM)
                query = rows[group, (b + 1) * SHIFT : (b + 2) * SHIFT, lanes]
                key = rows[group, span, width + h * HEAD_DIM : width + (h + 1) * HEAD_DIM]
                value = rows[group, span, 2 * width + h * HEAD_DIM : 2 * width + (h + 1) * HEAD_DIM]
                scores = lax.dot_general(
                    query, key, (((1,), (1,)), ((), ())), preferred_element_type=jnp.float32
                ) * (1.0 / math.sqrt(HEAD_DIM))
                scores = jnp.where(allowed, scores, masked_out)
                exponent = jnp.exp(scores - jnp.max(scores, axis=-1, keepdims=True))
                total = jnp.sum(exponent, axis=-1, keepdims=True)
                weights = (exponent / total).astype(jnp.bfloat16)
                combined = jnp.dot(weights, value, preferred_element_type=jnp.float32)
                out[group, b * SHIFT : (b + 1) * SHIFT, lanes] = combined.astype(jnp.bfloat16)


def attend(flags, segs, heads, own, other, halo):
    tok_rows, features = own.shape
    vmem, smem = pl.BlockSpec(memory_space=pltpu.VMEM), pl.BlockSpec(memory_space=pltpu.SMEM)
    body = functools.partial(attend_kernel, tok_rows // SHIFT, heads)
    flops = 2 * tok_rows * 2 * SHIFT * HEAD_DIM * heads * 4
    return pl.pallas_call(
        body,
        out_shape=jax.ShapeDtypeStruct((2, tok_rows, heads * HEAD_DIM), jnp.bfloat16),
        in_specs=[smem] + [vmem] * 5,
        out_specs=vmem,
        scratch_shapes=[pltpu.VMEM((2, SHIFT + tok_rows, features), jnp.bfloat16)],
        compiler_params=pltpu.CompilerParams(vmem_limit_bytes=48 << 20),
        cost_estimate=pl.CostEstimate(flops=flops, bytes_accessed=8 << 20, transcendentals=0),
    )(flags, segs[:, None, :], segs[:, :, None], own, other, halo)


def finish(attended, own_part, blocks, places):
    plane, count, depth, columns = blocks.shape
    rows = own_part.shape[0]
    wide = count + 1
    halves = 2

    def body(places, attended, own_part, block, out, total):
        s, k = pl.program_id(0), pl.program_id(1)

        @pl.when(s == 0)
        def _():
            out[...] = own_part[...]

        @pl.when(s > 0)
        def _():
            part = jnp.zeros((rows, columns), jnp.float32)
            for p in range(plane // halves):
                part += jnp.dot(attended[p], block[p, 0], preferred_element_type=jnp.float32)

            @pl.when(k == 0)
            def _():
                total[...] = part

            @pl.when(k > 0)
            def _():
                out[...] = (total[...] + part).astype(out.dtype)

    def block_at(s, k, places):
        return jnp.where(s > 0, k, 0), jnp.maximum(s - 1, 0), 0, 0

    return pl.pallas_call(
        body,
        out_shape=jax.ShapeDtypeStruct((rows, wide * columns), jnp.bfloat16),
        grid_spec=pltpu.PrefetchScalarGridSpec(
            num_scalar_prefetch=1,
            grid=(wide, halves),
            in_specs=[
                pl.BlockSpec((plane // halves, rows, depth), lambda s, k, places: (k, 0, 0)),
                pl.BlockSpec((rows, columns), lambda s, k, places: (0, 0)),
                pl.BlockSpec((plane // halves, 1, depth, columns), block_at),
            ],
            out_specs=pl.BlockSpec((rows, columns), lambda s, k, places: (0, places[s])),
            scratch_shapes=[pltpu.VMEM((rows, columns), jnp.float32)],
        ),
        compiler_params=pltpu.CompilerParams(vmem_limit_bytes=48 << 20),
    )(places, attended, own_part, blocks)


def per_device(hidden, w_qkv, w_out, seg_ids, shift_heads):
    tok_rows, depth = hidden.shape
    wide, narrow, groups = lax.axis_size("wide"), lax.axis_size("narrow"), lax.axis_size("groups")
    wide_idx, narrow_idx, group_idx = (lax.axis_index(a) for a in ("wide", "narrow", "groups"))
    in_rows, _, block_f = w_qkv.shape
    local_f = block_f // groups
    heads_here = local_f // HEAD_DIM
    plane = narrow * groups
    masks = [narrow >> (k + 1) for k in range(narrow.bit_length() - 1)]
    y_route = xor_route(groups, 1)

    def rel(e, steps):
        return sum(m for k, m in enumerate(steps) if (e >> k) & 1)

    halo_rows = SHIFT // narrow
    half = tok_rows // 2
    side = narrow_idx % 2

    def rows_of(start, count):
        return lax.dynamic_slice_in_dim(hidden, start, count, 0)

    def spread(stack, some, *earlier):
        for m in some:
            more = send(stack, "narrow", xor_route(narrow, m), *earlier)
            stack = jnp.concatenate([stack, more], 0)
        return stack

    def line_step(step, up, down, *earlier):
        up = send(up, "wide", [(i, i + 1) for i in range(step - 1, wide - 1)], *earlier)
        down = send(down, "wide", [(i, i - 1) for i in range(1, wide - step + 1)], *earlier)
        return up, down

    out_piece = lax.dynamic_slice_in_dim(w_out, (narrow_idx * groups + group_idx) * local_f, local_f, 0)
    line = [(out_piece, out_piece)]
    line.append(line_step(1, *line[0]))
    own_w = lax.dynamic_slice_in_dim(w_qkv, group_idx * local_f, local_f, 2)
    own_w = jnp.concatenate([own_w[:, 0], own_w[:, 1], own_w[:, 2]], 1)
    size = min(in_rows, CHUNK_ROWS)
    chunks = in_rows // size
    held = [[(own_w[c * size : (c + 1) * size],) * 2] for c in range(chunks)]
    held[0].append(line_step(1, *held[0][0]))
    other = send(rows_of(side * half, half), "groups", y_route)
    halo = send(
        rows_of(tok_rows - SHIFT + narrow_idx * halo_rows, halo_rows),
        "wide",
        [(i, (i + 1) % wide) for i in range(wide)],
        *line[1],
    )
    for step in range(2, wide):
        line.append(line_step(step, *line[-1], *(held[0][1] if step == 3 else ())))
    for c in range(1, chunks):
        held[c].append(line_step(1, *held[c][0], *line[min(2, wide - 1)]))
    pieces = []
    for d in range(1, wide):
        pieces.append(jnp.where(wide_idx + d < wide, line[d][1], line[wide - d][0]))
    halo_y = send(halo, "groups", y_route)
    other_seg = lax.ppermute(seg_ids, "groups", y_route)
    early = (other, halo_y, other_seg, *held[0][1], *held[-1][1])
    out_blocks = lax.all_gather(after(jnp.stack(pieces), *early), ("groups", "narrow"), axis=0)
    other = spread(other[None], [1])
    halos = spread(jnp.stack([halo, halo_y])[None], masks)

    arrived = [(wide_idx, 0, own_w)]
    for step in range(1, wide):
        for c in range(chunks):
            if step > 1:
                held[c].append(line_step(step, *held[c][-1]))
            up, down = held[c][step]
            below, above = wide_idx - step, wide_idx + step
            low, high = jnp.maximum(below, 0), jnp.minimum(above, wide - 1)
            if 2 * step <= wide - 1:
                arrived += [(low, c * size, up), (high, c * size, down)]
            else:
                arrived.append(
                    (jnp.where(below >= 0, low, high), c * size, jnp.where(below >= 0, up, down))
                )

    def project(rows):
        flat = rows.reshape(-1, depth)
        total = None
        for owner, first, block in arrived:
            columns = lax.dynamic_slice_in_dim(flat, owner * in_rows + first, block.shape[0], 1)
            product = jnp.dot(columns, block, preferred_element_type=jnp.float32)
            total = product if total is None else lax.optimization_barrier(total + product)
        return total.astype(jnp.bfloat16)

    sets = [project(r) for r in (hidden, other, halos)]

    segs = jnp.stack([seg_ids, other_seg])
    segs = jnp.concatenate([segs[:, -SHIFT:], segs], 1)
    shifted = lax.dynamic_slice_in_dim(
        shift_heads, (narrow_idx * groups + group_idx) * heads_here, heads_here
    )

    def entry_of(distance):
        return sum(((distance // m) % 2) * (1 << k) for k, m in enumerate(masks))

    entries = [entry_of(narrow_idx ^ b) for b in range(narrow)]
    flags = jnp.concatenate([jnp.stack([side] + entries), shifted > 0]).astype(jnp.int32)
    segs = lax.dynamic_slice_in_dim(segs, wide_idx * tok_rows, SHIFT + tok_rows, 1)
    attended = attend(flags, segs, heads_here, *sets)

    out_rows = tok_rows // narrow
    to_all = attended.reshape(2, narrow, out_rows, local_f)
    to_all = jnp.where(group_idx == 0, to_all, to_all[::-1]).reshape(plane * out_rows, local_f)
    from_all = lax.all_to_all(to_all, ("groups", "narrow"), 0, 0, tiled=True)
    in_order = from_all.reshape(groups, narrow, out_rows, local_f).transpose(2, 1, 0, 3)
    own_part = jnp.dot(
        in_order.reshape(out_rows, -1), w_out, preferred_element_type=jnp.float32
    ).astype(jnp.bfloat16)
    places = jnp.stack([(wide_idx + d) % wide for d in range(wide)]).astype(jnp.int32)
    return finish(from_all.reshape(plane, out_rows, local_f), own_part, out_blocks, places)


def solution(mesh):
    placed = (
        P(("groups", "wide"), None),
        P("wide", None, "narrow"),
        P(None, "wide"),
        P("groups"),
        P(),
    )
    return jax.shard_map(
        per_device,
        mesh=mesh,
        in_specs=placed,
        out_specs=P(("groups", "wide", "narrow"), None),
        check_vma=False,
    )
```

```python
import functools
import math

import jax
import jax.numpy as jnp
from jax import lax
from jax.experimental import pallas as pl
from jax.experimental.pallas import tpu as pltpu
from jax.sharding import PartitionSpec as P

HEAD_DIM = 128
GROUP = 512
SHIFT = 256
CHUNK_ROWS = 512

masked_out = -1e30
O = {'other': 0, 'seg': 0, 'c01': 0, 'halo': 1, 'w2way': 0, 'w2': 0, 'c11': 3, 'w3': 1, 'c2way': 0, 'c02': 0, 'halo_y': 0, 'halox': 0, 'gate': 59, 'othercore': 0, 'c12': 0, 'c03': 0, 'c13': 0, 'size': 0, 'tail': 1, 'owntie': 2}


def after(block, *earlier):
    return lax.optimization_barrier((block, *earlier))[0]


def send(block, axis, route, *earlier):
    if earlier:
        block = after(block, *earlier)
    return lax.ppermute(block, axis, route)


def xor_route(size, mask):
    return [(i, i ^ mask) for i in range(size)]


def attend_kernel(blocks, heads, flags, row_seg, col_seg, own, other, halo, out, rows):
    narrow = flags.shape[0] - 1 - heads
    tok_rows = own.shape[0]
    half = tok_rows // 2
    halo_rows = SHIFT // narrow
    for group in range(2):
        for b in range(narrow):
            place = pl.multiple_of((flags[1 + b] * 2 + group) * halo_rows, halo_rows)
            rows[group, b * halo_rows : (b + 1) * halo_rows] = halo[pl.ds(place, halo_rows)]
    rows[0, SHIFT:] = own[...]
    for b in range(2):
        place = pl.multiple_of((b ^ flags[0]) * half, half)
        rows[1, SHIFT + b * half : SHIFT + (b + 1) * half] = other[pl.ds(place, half)]

    i = lax.broadcasted_iota(jnp.int32, (SHIFT, 2 * SHIFT), 0)
    j = lax.broadcasted_iota(jnp.int32, (SHIFT, 2 * SHIFT), 1) - SHIFT
    width = heads * HEAD_DIM
    for group in range(2):
        for b in range(blocks):
            span = slice(b * SHIFT, (b + 2) * SHIFT)
            same = col_seg[group, (b + 1) * SHIFT : (b + 2) * SHIFT] == row_seg[group, :, span]
            causal = same & (j >= 0) & (j <= i)
            whole = same & (j < 0)
            for h in range(heads):
                joined = flags[1 + narrow + h] != b % (GROUP // SHIFT)
                allowed = causal | (whole & joined)
                lanes = slice(h * HEAD_DIM, (h + 1) * HEAD_DIM)
                query = rows[group, (b + 1) * SHIFT : (b + 2) * SHIFT, lanes]
                key = rows[group, span, width + h * HEAD_DIM : width + (h + 1) * HEAD_DIM]
                value = rows[group, span, 2 * width + h * HEAD_DIM : 2 * width + (h + 1) * HEAD_DIM]
                scores = lax.dot_general(
                    query, key, (((1,), (1,)), ((), ())), preferred_element_type=jnp.float32
                ) * (1.0 / math.sqrt(HEAD_DIM))
                scores = jnp.where(allowed, scores, masked_out)
                exponent = jnp.exp(scores - jnp.max(scores, axis=-1, keepdims=True))
                total = jnp.sum(exponent, axis=-1, keepdims=True)
                weights = (exponent / total).astype(jnp.bfloat16)
                combined = jnp.dot(weights, value, preferred_element_type=jnp.float32)
                out[group, b * SHIFT : (b + 1) * SHIFT, lanes] = combined.astype(jnp.bfloat16)


def attend(flags, segs, heads, own, other, halo):
    tok_rows, features = own.shape
    vmem, smem = pl.BlockSpec(memory_space=pltpu.VMEM), pl.BlockSpec(memory_space=pltpu.SMEM)
    body = functools.partial(attend_kernel, tok_rows // SHIFT, heads)
    flops = 2 * tok_rows * 2 * SHIFT * HEAD_DIM * heads * 4
    return pl.pallas_call(
        body,
        out_shape=jax.ShapeDtypeStruct((2, tok_rows, heads * HEAD_DIM), jnp.bfloat16),
        in_specs=[smem] + [vmem] * 5,
        out_specs=vmem,
        scratch_shapes=[pltpu.VMEM((2, SHIFT + tok_rows, features), jnp.bfloat16)],
        compiler_params=pltpu.CompilerParams(vmem_limit_bytes=48 << 20),
        cost_estimate=pl.CostEstimate(flops=flops, bytes_accessed=8 << 20, transcendentals=0),
    )(flags, segs[:, None, :], segs[:, :, None], own, other, halo)


def finish(attended, own_block, blocks, places, narrow):
    plane, count, depth, columns = blocks.shape
    rows = attended.shape[1]
    groups = plane // narrow

    def body(places, attended, own_block, block, out):
        s = pl.program_id(0)

        @pl.when(s == 0)
        def _():
            order = [(b % groups) * narrow + b // groups for b in range(plane)]
            mine = jnp.concatenate([attended[p] for p in order], 1)
            value = jnp.dot(mine, own_block[...], preferred_element_type=jnp.float32)
            out[...] = value.astype(out.dtype)

        @pl.when(s > 0)
        def _():
            mine = jnp.concatenate([attended[p] for p in range(plane)], 1)
            weights = block[...].reshape(plane * depth, columns)
            value = jnp.dot(mine, weights, preferred_element_type=jnp.float32)
            out[...] = value.astype(out.dtype)

    return pl.pallas_call(
        body,
        out_shape=jax.ShapeDtypeStruct((rows, (count + 1) * columns), jnp.bfloat16),
        grid_spec=pltpu.PrefetchScalarGridSpec(
            num_scalar_prefetch=1,
            grid=(count + 1,),
            in_specs=[
                pl.BlockSpec((plane, rows, depth), lambda s, places: (0, 0, 0)),
                pl.BlockSpec((plane * depth, columns), lambda s, places: (0, 0)),
                pl.BlockSpec(
                    (plane, 1, depth, columns),
                    lambda s, places: (0, jnp.maximum(s - 1, 0), 0, 0),
                ),
            ],
            out_specs=pl.BlockSpec((rows, columns), lambda s, places: (0, places[s])),
        ),
        compiler_params=pltpu.CompilerParams(vmem_limit_bytes=48 << 20),
    )(places, attended, own_block, blocks)


def per_device(hidden, w_qkv, w_out, seg_ids, shift_heads):
    tok_rows, depth = hidden.shape
    wide, narrow, groups = lax.axis_size("wide"), lax.axis_size("narrow"), lax.axis_size("groups")
    wide_idx, narrow_idx, group_idx = (lax.axis_index(a) for a in ("wide", "narrow", "groups"))
    in_rows, _, block_f = w_qkv.shape
    local_f = block_f // groups
    heads_here = local_f // HEAD_DIM
    plane = narrow * groups
    masks = [narrow >> (k + 1) for k in range(narrow.bit_length() - 1)]
    y_route = xor_route(groups, 1)

    def rel(e, steps):
        return sum(m for k, m in enumerate(steps) if (e >> k) & 1)

    halo_rows = SHIFT // narrow
    half = tok_rows // 2
    side = narrow_idx % 2

    def rows_of(start, count):
        return lax.dynamic_slice_in_dim(hidden, start, count, 0)

    def spread(stack, some, *earlier):
        for m in some:
            more = send(stack, "narrow", xor_route(narrow, m), *earlier)
            stack = jnp.concatenate([stack, more], 0)
        return stack

    lone = wide // 2

    def both_ways(block, hops, *earlier):
        up = send(block, "wide", [(i, i + hops) for i in range(wide - hops)], *earlier)
        down = send(block, "wide", [(i, i - hops) for i in range(hops, wide)], *earlier)
        return up, down

    def select(step, pair):
        return (jnp.where(wide_idx >= step, *pair),) * 2 if step == lone else pair

    def onward(step, pair, *earlier):
        up = [(i, i + 1) for i in range(step - 1, wide - 1)]
        down = [(i, i - 1) for i in range(1, wide - step + 1)]
        if step > lone:
            return (send(pair[0], "wide", up + down, *earlier),) * 2
        return select(
            step, (send(pair[0], "wide", up, *earlier), send(pair[1], "wide", down, *earlier))
        )

    out_piece = lax.dynamic_slice_in_dim(w_out, (narrow_idx * groups + group_idx) * local_f, local_f, 0)
    own_w = lax.dynamic_slice_in_dim(w_qkv, group_idx * local_f, local_f, 2)
    own_w = jnp.concatenate([own_w[:, 0], own_w[:, 1], own_w[:, 2]], 1)
    size = min(in_rows, CHUNK_ROWS)
    chunks = in_rows // size
    own_chunks = [own_w[c * size : (c + 1) * size] for c in range(chunks)]

    def pick(name, *choices):
        return choices[O[name]]

    def step_two(block, first, way, *ties):
        if way:
            return select(2, both_ways(block, 2, *ties))
        return onward(2, first, *ties)

    line = {1: select(1, both_ways(out_piece, 1))}
    held = [{} for _ in range(chunks)]
    other = send(rows_of(side * half, half), "groups", y_route, *pick("other", (), line[1]))
    other_seg = send(seg_ids, "groups", y_route, *pick("seg", (), line[1], (other,)))
    held[0][1] = select(1, both_ways(own_chunks[0], 1, *pick("c01", (), line[1])))
    halo = send(
        rows_of(tok_rows - SHIFT + narrow_idx * halo_rows, halo_rows),
        "wide",
        [(i, (i + 1) % wide) for i in range(wide)],
        *pick("halo", (), line[1], held[0][1]),
    )
    line[2] = step_two(out_piece, line[1], O["w2way"], *pick("w2", (), held[0][1], line[1]))
    for c in range(1, chunks):
        held[c][1] = select(1, both_ways(own_chunks[c], 1, *pick("c11", (), line[1], held[0][1], line[2])))
    for step in range(3, wide):
        line[step] = onward(
            step, line[step - 1], *pick("w3", (), held[0][1], (other,), (other, *held[0][1]), held[-1][1], (halo, *held[0][1]))
        )
    last = line[wide - 1]
    held[0][2] = step_two(own_chunks[0], held[0][1], O["c2way"], *pick("c02", (), line[2], last, held[-1][1]))
    halo_y = send(halo, "groups", y_route, *pick("halo_y", (), (other,)))
    halos = spread(jnp.stack([halo, halo_y])[None], masks[:-1], *pick("halox", (), last, held[-1][1], line[2]))
    pieces = []
    for d in range(1, wide):
        pieces.append(jnp.where(wide_idx + d < wide, line[d][1], line[wide - d][0]))
    gates = [(other,), (halo_y,), (halos,), (other_seg,), held[0][1], held[-1][1], held[0][2]]
    early = [x for bit, g in enumerate(gates) if (O["gate"] >> bit) & 1 for x in g]
    out_blocks = lax.all_gather(after(jnp.stack(pieces), *early), ("groups", "narrow"), axis=0)
    other = spread(other[None], [1], *pick("othercore", (), last, held[-1][1]))
    halos = spread(halos, masks[-1:])
    for c in range(1, chunks):
        held[c][2] = step_two(
            own_chunks[c], held[c][1], O["c2way"], *pick("c12", (), held[0][2], (other,), (last[0], other))
        )

    own_tied = pick("owntie", (), held[0][2], held[-1][1])
    weights = [(wide_idx, 0, after(own_w, *own_tied) if own_tied else own_w)]
    row_sets = [hidden, other, halos]
    sums, taken = [None] * 3, [0] * 3

    def project(k, count=None):
        flat = row_sets[k].reshape(-1, depth)
        for owner, start, block in weights[taken[k] : count]:
            columns = lax.dynamic_slice_in_dim(flat, owner * in_rows + start, block.shape[0], 1)
            product = jnp.dot(columns, block, preferred_element_type=jnp.float32)
            if sums[k] is None:
                sums[k] = product
            else:
                sums[k] = lax.optimization_barrier(sums[k] + product)
        taken[k] = len(weights) if count is None else max(count, taken[k])
        return sums[k]

    def take(c, step):
        below, above = wide_idx - step, wide_idx + step
        low, high = jnp.maximum(below, 0), jnp.minimum(above, wide - 1)
        up, down = held[c][step]
        if step < lone:
            weights.extend([(low, c * size, up), (high, c * size, down)])
        else:
            weights.append((jnp.where(below >= 0, low, high), c * size, up))

    for c in range(chunks):
        take(c, 1)
    near = len(weights)
    for c in range(chunks):
        take(c, 2)
    for step in range(3, wide):
        for c in range(chunks):
            if c == 0:
                ready = [(), lambda: (project(0, near),), lambda: (project(0, near), other)][O["c03"]]
            else:
                known = near + 1
                ready = [
                    (),
                    lambda: (project(0, known),),
                    lambda: (project(0, known), project(1, known)),
                    lambda: (project(0, known), project(1, known), halos),
                    lambda: (project(0, near), project(1, near)),
                ][O["c13"]]
            ready = ready() if callable(ready) else ready
            pair = onward(step, held[c][step - 1], *ready)
            if step == wide - 1 and c == chunks - 1 and O["tail"]:
                known = [project(k) for k in range(3)]
                pair = (after(pair[0], *known),) * 2
            held[c][step] = pair
            take(c, step)
    sets = [project(k).astype(jnp.bfloat16) for k in range(3)]

    segs = jnp.stack([seg_ids, other_seg])
    segs = jnp.concatenate([segs[:, -SHIFT:], segs], 1)
    shifted = lax.dynamic_slice_in_dim(
        shift_heads, (narrow_idx * groups + group_idx) * heads_here, heads_here
    )

    def entry_of(distance):
        return sum(((distance // m) % 2) * (1 << k) for k, m in enumerate(masks))

    entries = [entry_of(narrow_idx ^ b) for b in range(narrow)]
    flags = jnp.concatenate([jnp.stack([side] + entries), shifted > 0]).astype(jnp.int32)
    segs = lax.dynamic_slice_in_dim(segs, wide_idx * tok_rows, SHIFT + tok_rows, 1)
    attended = attend(flags, segs, heads_here, *sets)

    out_rows = tok_rows // narrow
    to_all = attended.reshape(2, narrow, out_rows, local_f)
    to_all = jnp.where(group_idx == 0, to_all, to_all[::-1]).reshape(plane * out_rows, local_f)
    from_all = lax.all_to_all(to_all, ("groups", "narrow"), 0, 0, tiled=True)
    places = jnp.stack([(wide_idx + d) % wide for d in range(wide)]).astype(jnp.int32)
    return finish(
        from_all.reshape(plane, out_rows, local_f), w_out, out_blocks, places, narrow
    )


def solution(mesh):
    placed = (
        P(("groups", "wide"), None),
        P("wide", None, "narrow"),
        P(None, "wide"),
        P("groups"),
        P(),
    )
    return jax.shard_map(
        per_device,
        mesh=mesh,
        in_specs=placed,
        out_specs=P(("groups", "wide", "narrow"), None),
        check_vma=False,
    )
```

```python
import functools
import math

import jax
import jax.numpy as jnp
from jax import lax
from jax.experimental import pallas as pl
from jax.experimental.pallas import tpu as pltpu
from jax.sharding import PartitionSpec as P

HEAD_DIM = 128
GROUP = 512
SHIFT = 256
CHUNK_ROWS = 512

masked_out = -1e30
O = {'other': 0, 'seg': 0, 'c01': 0, 'halo': 2, 'w2way': 0, 'w2': 0, 'c11': 3, 'w3': 3, 'c2way': 0, 'c02': 0, 'halo_y': 0, 'halox': 0, 'gate': 31, 'othercore': 0, 'c12': 0, 'c03': 0, 'c13': 0, 'size': 0, 'tail': 1, 'owntie': 1, 'st1': 1, 'st2': 2, 'otherb': 0}


def after(block, *earlier):
    return lax.optimization_barrier((block, *earlier))[0]


def send(block, axis, route, *earlier):
    if earlier:
        block = after(block, *earlier)
    return lax.ppermute(block, axis, route)


def xor_route(size, mask):
    return [(i, i ^ mask) for i in range(size)]


def attend_kernel(blocks, heads, flags, row_seg, col_seg, own, other, halo, out, rows):
    narrow = flags.shape[0] - 2 - heads
    tok_rows = own.shape[0]
    half = tok_rows // 2
    halo_rows = SHIFT // narrow
    for group in range(2):
        for b in range(narrow):
            place = pl.multiple_of((flags[1 + b] * 2 + group) * halo_rows, halo_rows)
            rows[group, b * halo_rows : (b + 1) * halo_rows] = halo[pl.ds(place, halo_rows)]
    rows[0, SHIFT:] = own[...]
    for b in range(2):
        place = pl.multiple_of((b ^ flags[0]) * half, half)
        rows[1, SHIFT + b * half : SHIFT + (b + 1) * half] = other[pl.ds(place, half)]

    i = lax.broadcasted_iota(jnp.int32, (SHIFT, 2 * SHIFT), 0)
    j = lax.broadcasted_iota(jnp.int32, (SHIFT, 2 * SHIFT), 1) - SHIFT
    width = heads * HEAD_DIM
    for group in range(2):
        place = flags[1 + narrow + heads] ^ group
        for b in range(blocks):
            span = slice(b * SHIFT, (b + 2) * SHIFT)
            same = col_seg[group, (b + 1) * SHIFT : (b + 2) * SHIFT] == row_seg[group, :, span]
            causal = same & (j >= 0) & (j <= i)
            whole = same & (j < 0)
            for h in range(heads):
                joined = flags[1 + narrow + h] != b % (GROUP // SHIFT)
                allowed = causal | (whole & joined)
                lanes = slice(h * HEAD_DIM, (h + 1) * HEAD_DIM)
                query = rows[group, (b + 1) * SHIFT : (b + 2) * SHIFT, lanes]
                key = rows[group, span, width + h * HEAD_DIM : width + (h + 1) * HEAD_DIM]
                value = rows[group, span, 2 * width + h * HEAD_DIM : 2 * width + (h + 1) * HEAD_DIM]
                scores = lax.dot_general(
                    query, key, (((1,), (1,)), ((), ())), preferred_element_type=jnp.float32
                ) * (1.0 / math.sqrt(HEAD_DIM))
                scores = jnp.where(allowed, scores, masked_out)
                exponent = jnp.exp(scores - jnp.max(scores, axis=-1, keepdims=True))
                total = jnp.sum(exponent, axis=-1, keepdims=True)
                weights = (exponent / total).astype(jnp.bfloat16)
                combined = jnp.dot(weights, value, preferred_element_type=jnp.float32)
                out[place, b * SHIFT : (b + 1) * SHIFT, lanes] = combined.astype(jnp.bfloat16)


def attend(flags, segs, heads, own, other, halo):
    tok_rows, features = own.shape
    vmem, smem = pl.BlockSpec(memory_space=pltpu.VMEM), pl.BlockSpec(memory_space=pltpu.SMEM)
    body = functools.partial(attend_kernel, tok_rows // SHIFT, heads)
    flops = 2 * tok_rows * 2 * SHIFT * HEAD_DIM * heads * 4
    return pl.pallas_call(
        body,
        out_shape=jax.ShapeDtypeStruct((2, tok_rows, heads * HEAD_DIM), jnp.bfloat16),
        in_specs=[smem] + [vmem] * 5,
        out_specs=vmem,
        scratch_shapes=[pltpu.VMEM((2, SHIFT + tok_rows, features), jnp.bfloat16)],
        compiler_params=pltpu.CompilerParams(vmem_limit_bytes=48 << 20),
        cost_estimate=pl.CostEstimate(flops=flops, bytes_accessed=8 << 20, transcendentals=0),
    )(flags, segs[:, None, :], segs[:, :, None], own, other, halo)


def finish(attended, own_block, parts, orders, places, narrow):
    _, count, depth, columns = parts[0][0].shape
    plane, rows, _ = attended.shape
    groups = plane // narrow
    cut = plane // 4

    def body(places, first, second, attended, own, a0, a1, a2, a3, b0, b1, b2, b3, out, held, arrival):
        s = pl.program_id(0)
        copy = pltpu.make_async_copy(own, held, arrival)

        @pl.when(s == 0)
        def _():
            copy.start()

        @pl.when(s < count)
        def _():
            value = jnp.zeros((rows, columns), jnp.float32)
            for h, (table, pair) in enumerate(
                ((first, (a0, a1, a2, a3)), (second, (b0, b1, b2, b3)))
            ):
                for p, block in enumerate(pair):
                    mine = [
                        attended[table[p * cut + e]][:, h * depth : (h + 1) * depth]
                        for e in range(cut)
                    ]
                    value += jnp.dot(
                        jnp.concatenate(mine, 1),
                        block[...].reshape(cut * depth, columns),
                        preferred_element_type=jnp.float32,
                    )
            out[...] = value.astype(out.dtype)

        @pl.when(s == count)
        def _():
            copy.wait()
            order = [(b % groups) * narrow + b // groups for b in range(plane)]
            mine = jnp.concatenate([attended[p] for p in order], 1)
            value = jnp.dot(mine, held[...], preferred_element_type=jnp.float32)
            out[...] = value.astype(out.dtype)

    piece = pl.BlockSpec((cut, 1, depth, columns), lambda s, *_: (0, jnp.minimum(s, count - 1), 0, 0))
    return pl.pallas_call(
        body,
        out_shape=jax.ShapeDtypeStruct((rows, (count + 1) * columns), jnp.bfloat16),
        grid_spec=pltpu.PrefetchScalarGridSpec(
            num_scalar_prefetch=3,
            grid=(count + 1,),
            in_specs=[
                pl.BlockSpec(attended.shape, lambda s, *_: (0, 0, 0)),
                pl.BlockSpec(memory_space=pl.ANY),
                *[piece] * 8,
            ],
            out_specs=pl.BlockSpec((rows, columns), lambda s, places, *_: (0, places[s])),
            scratch_shapes=[pltpu.VMEM(own_block.shape, own_block.dtype), pltpu.SemaphoreType.DMA],
        ),
        compiler_params=pltpu.CompilerParams(vmem_limit_bytes=60 << 20),
    )(places, *orders, attended, own_block, *parts[0], *parts[1])


def per_device(hidden, w_qkv, w_out, seg_ids, shift_heads):
    tok_rows, depth = hidden.shape
    wide, narrow, groups = lax.axis_size("wide"), lax.axis_size("narrow"), lax.axis_size("groups")
    wide_idx, narrow_idx, group_idx = (lax.axis_index(a) for a in ("wide", "narrow", "groups"))
    in_rows, _, block_f = w_qkv.shape
    local_f = block_f // groups
    heads_here = local_f // HEAD_DIM
    plane = narrow * groups
    masks = [narrow >> (k + 1) for k in range(narrow.bit_length() - 1)]
    y_route = xor_route(groups, 1)

    def rel(e, steps):
        return sum(m for k, m in enumerate(steps) if (e >> k) & 1)

    halo_rows = SHIFT // narrow
    half = tok_rows // 2
    side = narrow_idx % 2

    def rows_of(start, count):
        return lax.dynamic_slice_in_dim(hidden, start, count, 0)

    def spread(stack, some, *earlier):
        for m in some:
            more = send(stack, "narrow", xor_route(narrow, m), *earlier)
            stack = jnp.concatenate([stack, more], 0)
        return stack

    lone = wide // 2

    def both_ways(block, hops, *earlier):
        up = send(block, "wide", [(i, i + hops) for i in range(wide - hops)], *earlier)
        down = send(block, "wide", [(i, i - hops) for i in range(hops, wide)], *earlier)
        return up, down

    def select(step, pair):
        return (jnp.where(wide_idx >= step, *pair),) * 2 if step == lone else pair

    def onward(step, pair, *earlier):
        up = [(i, i + 1) for i in range(step - 1, wide - 1)]
        down = [(i, i - 1) for i in range(1, wide - step + 1)]
        if step > lone:
            return (send(pair[0], "wide", up + down, *earlier),) * 2
        return select(
            step, (send(pair[0], "wide", up, *earlier), send(pair[1], "wide", down, *earlier))
        )

    out_piece = lax.dynamic_slice_in_dim(w_out, (narrow_idx * groups + group_idx) * local_f, local_f, 0)
    own_w = lax.dynamic_slice_in_dim(w_qkv, group_idx * local_f, local_f, 2)
    own_w = jnp.concatenate([own_w[:, 0], own_w[:, 1], own_w[:, 2]], 1)
    size = min(in_rows, CHUNK_ROWS)
    chunks = in_rows // size
    own_chunks = [own_w[c * size : (c + 1) * size] for c in range(chunks)]

    def pick(name, *choices):
        return choices[O[name]]

    def step_two(block, first, way, *ties):
        if way:
            return select(2, both_ways(block, 2, *ties))
        return onward(2, first, *ties)

    line = {1: select(1, both_ways(out_piece, 1))}
    held = [{} for _ in range(chunks)]
    other = send(rows_of(side * half, half), "groups", y_route, *pick("other", (), line[1]))
    other_seg = send(seg_ids, "groups", y_route, *pick("seg", (), line[1], (other,)))
    held[0][1] = select(1, both_ways(own_chunks[0], 1, *pick("c01", (), line[1])))
    halo = send(
        rows_of(tok_rows - SHIFT + narrow_idx * halo_rows, halo_rows),
        "wide",
        [(i, (i + 1) % wide) for i in range(wide)],
        *pick("halo", (), line[1], held[0][1]),
    )
    line[2] = step_two(out_piece, line[1], O["w2way"], *pick("w2", (), held[0][1], line[1]))
    for c in range(1, chunks):
        held[c][1] = select(1, both_ways(own_chunks[c], 1, *pick("c11", (), line[1], held[0][1], line[2])))
    for step in range(3, wide):
        line[step] = onward(
            step, line[step - 1], *pick("w3", (), held[0][1], (other,), (other, *held[0][1]), held[-1][1], (halo, *held[0][1]))
        )
    last = line[wide - 1]
    held[0][2] = step_two(own_chunks[0], held[0][1], O["c2way"], *pick("c02", (), line[2], last, held[-1][1]))
    halo_y = send(halo, "groups", y_route, *pick("halo_y", (), (other,)))
    halos = spread(jnp.stack([halo, halo_y])[None], masks[:-1], *pick("halox", (), last, held[-1][1], line[2]))
    pieces = []
    for d in range(1, wide):
        pieces.append(jnp.where(wide_idx + d < wide, line[d][1], line[wide - d][0]))
    gates = [(other,), (halo_y,), (halos,), (other_seg,), held[0][1], held[-1][1], held[0][2]]
    early = [x for bit, g in enumerate(gates) if (O["gate"] >> bit) & 1 for x in g]
    stack = after(jnp.stack(pieces), *early)
    middle = stack.shape[1] // 2
    hops = [("groups", y_route, narrow)]
    hops += [("narrow", xor_route(narrow, m), m) for m in masks]
    walks = [hops, hops[1:2] + hops[:1] + hops[2:]]
    halves = [stack[None, :, :middle], stack[None, :, middle:]]
    for hop in range(len(hops) - 2):
        for h in range(2):
            halves[h] = jnp.concatenate([halves[h], send(halves[h], *walks[h][hop][:2])], 0)
    stages = [tuple(halves)]
    passed = [send(halves[h], *walks[h][-2][:2]) for h in range(2)]
    stages.append(tuple(passed))
    parts = []
    for half, more in zip(halves, passed):
        parts.append((half, more, send(half, *hops[-1][:2]), send(more, *hops[-1][:2])))
    tables = [
        jnp.stack(
            [
                (group_idx * narrow + narrow_idx) ^ rel(e, [m for _, _, m in walk])
                for e in range(plane)
            ]
        ).astype(jnp.int32)
        for walk in walks
    ]
    other = spread(other[None], [1], *pick("othercore", (), last, held[-1][1]))
    halos = spread(halos, masks[-1:])
    for c in range(1, chunks):
        held[c][2] = step_two(
            own_chunks[c], held[c][1], O["c2way"], *pick("c12", (), held[0][2], (other,), (last[0], other))
        )

    own_tied = pick("owntie", (), held[0][2], held[-1][1])
    weights = [(wide_idx, 0, after(own_w, *own_tied) if own_tied else own_w)]
    row_sets = [hidden, other, halos]
    sums, taken = [None] * 3, [0] * 3

    def project(k, count=None):
        flat = row_sets[k].reshape(-1, depth)
        for owner, start, block in weights[taken[k] : count]:
            columns = lax.dynamic_slice_in_dim(flat, owner * in_rows + start, block.shape[0], 1)
            product = jnp.dot(columns, block, preferred_element_type=jnp.float32)
            if sums[k] is None:
                sums[k] = product
            else:
                sums[k] = lax.optimization_barrier(sums[k] + product)
        taken[k] = len(weights) if count is None else max(count, taken[k])
        return sums[k]

    def take(c, step):
        below, above = wide_idx - step, wide_idx + step
        low, high = jnp.maximum(below, 0), jnp.minimum(above, wide - 1)
        up, down = held[c][step]
        if step < lone:
            weights.extend([(low, c * size, up), (high, c * size, down)])
        else:
            weights.append((jnp.where(below >= 0, low, high), c * size, up))

    for c in range(chunks):
        take(c, 1)
    near = len(weights)
    for c in range(chunks):
        take(c, 2)
    for step in range(3, wide):
        for c in range(chunks):
            if c == 0:
                ready = [(), lambda: (project(0, near),), lambda: (project(0, near), other)][O["c03"]]
            else:
                known = near + 1
                ready = [
                    (),
                    lambda: (project(0, known),),
                    lambda: (project(0, known), project(1, known)),
                    lambda: (project(0, known), project(1, known), halos),
                    lambda: (project(0, near), project(1, near)),
                ][O["c13"]]
            ready = ready() if callable(ready) else ready
            if step == wide - 1:
                ready += stages[0] if c == 0 and O["st1"] else ()
                ready += stages[-1] if c == chunks - 1 and O["st2"] == 1 else ()
            pair = onward(step, held[c][step - 1], *ready)
            if step == wide - 1 and c == chunks - 1 and O["tail"]:
                known = [project(k) for k in range(3)]
                pair = (after(pair[0], *known, *(stages[-1] if O["st2"] == 2 else ())),) * 2
            held[c][step] = pair
            take(c, step)
    sets = [project(k).astype(jnp.bfloat16) for k in range(3)]

    segs = jnp.stack([seg_ids, other_seg])
    segs = jnp.concatenate([segs[:, -SHIFT:], segs], 1)
    shifted = lax.dynamic_slice_in_dim(
        shift_heads, (narrow_idx * groups + group_idx) * heads_here, heads_here
    )

    def entry_of(distance):
        return sum(((distance // m) % 2) * (1 << k) for k, m in enumerate(masks))

    entries = [entry_of(narrow_idx ^ b) for b in range(narrow)]
    flags = jnp.concatenate([jnp.stack([side] + entries), shifted > 0, group_idx[None]]).astype(jnp.int32)
    segs = lax.dynamic_slice_in_dim(segs, wide_idx * tok_rows, SHIFT + tok_rows, 1)
    attended = attend(flags, segs, heads_here, *sets)

    out_rows = tok_rows // narrow
    to_all = attended.reshape(plane * out_rows, local_f)
    from_all = lax.all_to_all(to_all, ("groups", "narrow"), 0, 0, tiled=True)
    places = jnp.stack([(wide_idx + d) % wide for d in [*range(1, wide), 0]]).astype(jnp.int32)
    attended = from_all.reshape(plane, out_rows, local_f)
    return finish(attended, w_out, parts, tables, places, narrow)


def solution(mesh):
    placed = (
        P(("groups", "wide"), None),
        P("wide", None, "narrow"),
        P(None, "wide"),
        P("groups"),
        P(),
    )
    return jax.shard_map(
        per_device,
        mesh=mesh,
        in_specs=placed,
        out_specs=P(("groups", "wide", "narrow"), None),
        check_vma=False,
    )
```
